1024 devices in a mesh: sec: 4 (over x_lo), tile: 128 (over y, z, core), col: 2 (over x_hi).
Axes of the slice: x: 8 (x_hi: 2, x_lo: 4; x = x_hi * 4 + x_lo), y: 8, z: 8, core: 2. Of those that a mesh axis runs over, the one named last changes fastest.
Arguments:
- state: float32 [4, 8, 72, 256, 256], P('sec', None, None, 'tile', 'col'), may hold values from -6 to 6
- column_op: bfloat16 [4, 576, 576], P('sec'), may hold values from -0.125 to 0.125
- diffusion: float32 [4, 576], P('sec'), may hold values from 0.05 to 0.22
- remap_weights: bfloat16 [32, 128, 128], replicated, may hold values from -0.5 to 0.5
- source_rows: int32 [4, 256, 2, 4], P('sec', 'tile', 'col'), may hold values from 0 to 23, as said below
- weight_index: int32 [4, 256, 2, 4], P('sec', 'tile', 'col'), may hold values from 0 to 31
- intersection_count: int32 [4, 256, 2], P('sec', 'tile', 'col'), may hold values from 1 to 4, as said below
Outputs:
- state_next: float32 [4, 8, 72, 256, 256], P('sec', None, None, 'tile', 'col')
The draws below stay inside these ranges and needn't reach their ends.
Inputs may be any that keep to these rules, and one draw needn't show every extreme that they name: `source_rows`: each entry is s * 3 * 2 + (d + 1) * 2 + r for a source section s, a tile offset d of -1, 0 or 1 and a row r; blocks of the atmosphere sections (all but the last) take their sources from the last section only, blocks of the last section from the others only. Slots 0 to intersection_count - 1 of a block's list are live; every device holds a block with 4 live slots.
All inputs are finite; a program needn't handle non-finite values.
Results may differ from the reference program's by a relative error of at most 0.0017.
Values may be sent and summed in bfloat16 or wider, within the bound.
No kernel may reach another device: no remote copies, remote signals or barrier semaphores. Data moves between devices by JAX's collectives and lax.ppermute only.
A program may use at most 32 MiB of HBM per device.

```python
import math
import jax
import jax.numpy as jnp

VARS = 8
LEV = 72
BLK = 128
RX = 2
KMAX = 4
NW = 32
SUBSTEPS = 2
SECTIONS = 4
COLS = 2
NXG = 256
NYG = 256
VL = 576


def draw_source_rows(key, part):
    key = jax.random.fold_in(key, 11)
    first_key, second_key, third_key = jax.random.split(key, 3)
    dims_all = (SECTIONS, NXG, COLS, KMAX)
    sender = jax.random.randint(first_key, dims_all, 0, SECTIONS - 1)
    offset = jax.random.randint(second_key, dims_all, 0, 3)
    row_pick = jax.random.randint(third_key, dims_all, 0, RX)
    ocean_index = SECTIONS - 1
    is_ocean = (jnp.arange(SECTIONS) == ocean_index)[:, None, None, None]
    section = jnp.where(is_ocean, sender, ocean_index)
    entries = section * (3 * RX) + offset * RX + row_pick
    entries = entries.at[0, 0, 0, 0].set(SECTIONS * 3 * RX - 1)
    entries = entries.at[ocean_index, 0, 0, 0].set(0)
    return entries.astype(jnp.int32)


def draw_intersection_count(key, part):
    key = jax.random.fold_in(key, 12)
    counts = jax.random.randint(key, (SECTIONS, NXG, COLS), 1, KMAX + 1)
    filled = (jnp.arange(NXG) % RX == 0)[None, :, None]
    return jnp.where(filled, KMAX, counts).astype(jnp.int32)


def plant(array, rng, low, largest):
    extent = array.shape
    spot = [jax.random.randint(jax.random.fold_in(rng, axis), (), 0, extent[axis]) for axis in range(len(extent))]
    array = array.at[tuple(spot)].set(low)
    longest = extent.index(max(extent))
    spot[longest] = (spot[longest] + 1) % extent[longest]
    return array.at[tuple(spot)].set(largest)


def shard_levels(rng, extent, cuts, smallest, top_value):
    factor_of, own = 1.0, jax.random.fold_in(rng, 6)
    for dim, shards_of in cuts:
        steps = jnp.exp(jax.random.uniform(jax.random.fold_in(own, dim), (shards_of,), jnp.float32, smallest / len(cuts), top_value / len(cuts)))
        factor_of = factor_of * jnp.repeat(steps, extent[dim] // shards_of).reshape([-1 if axis == dim else 1 for axis in range(len(extent))])
    return factor_of


def bell_draw(rng, dims, width, bound, cuts=(), held_as=jnp.bfloat16):
    values = width * jax.random.normal(rng, dims, jnp.float32)
    if cuts:
        values = values * shard_levels(rng, dims, cuts, -0.22, 0.18)
    return jnp.clip(values, -bound, bound).astype(held_as)


def setup_inputs(seed: int = 0) -> dict:
    splits = jax.random.split(jax.random.key(seed), 8)
    return {
        "state": bell_draw(splits[0], (SECTIONS, VARS, LEV, NXG, NYG), 1.0, 6.0, ((0, 4), (3, 128), (4, 2)), jnp.float32),
        "column_op": bell_draw(splits[1], (SECTIONS, VL, VL), (4 * VL) ** -0.5, 0.125, ((0, 4),)),
        "diffusion": jnp.clip(jnp.exp(math.log(0.22) - 1.48160452 * jax.random.uniform(splits[2], (SECTIONS, VL), jnp.float32) ** shard_levels(splits[2], (SECTIONS, VL), ((0, 4),), -0.2, 0.2)), 0.05, 0.22),
        "remap_weights": bell_draw(splits[3], (NW, BLK, BLK), BLK ** -0.5, 0.5),
        "source_rows": draw_source_rows(jax.random.fold_in(splits[7], 71), 0),
        "weight_index": plant(jax.random.randint(splits[5], (SECTIONS, NXG, COLS, KMAX), 0, NW), jax.random.fold_in(splits[5], 1), 0, NW - 1).astype(jnp.int32),
        "intersection_count": draw_intersection_count(jax.random.fold_in(splits[7], 71), 0),
    }


def reference(state, column_op, diffusion, remap_weights, source_rows, weight_index, intersection_count):
    surface = state[:, :, 0].astype(jnp.bfloat16)
    surface_blocks = surface.reshape(SECTIONS, VARS, NXG, COLS, BLK)
    rows_all = jnp.arange(NXG, dtype=jnp.int32)[None, :, None]
    patches = jnp.arange(COLS, dtype=jnp.int32)[None, None, :]
    tiles_all = rows_all // RX
    tile_count = NXG // RX
    flux = jnp.zeros((SECTIONS, NXG, COLS, VARS, BLK), jnp.float32)
    for slot_index in range(KMAX):
        entry = source_rows[..., slot_index].astype(jnp.int32)
        section = entry // (3 * RX)
        within = entry % (3 * RX)
        offset = within // RX - 1
        source_x = ((tiles_all + offset) % tile_count) * RX + within % RX
        blocks = surface_blocks[section, :, source_x, patches].astype(jnp.float32)
        weights = remap_weights[weight_index[..., slot_index]].astype(jnp.float32)
        contrib = jnp.einsum("sxcvi,sxcij->sxcvj", blocks, weights)
        live = (slot_index < intersection_count)[..., None, None]
        flux = flux + jnp.where(live, contrib, jnp.float32(0.0))
    results = []
    for section_index in range(SECTIONS):
        field = state[section_index]
        spread_rate = diffusion[section_index].reshape(VARS, LEV, 1, 1)
        for substep in range(SUBSTEPS):
            laplace = (jnp.roll(field, -1, 2) + jnp.roll(field, 1, 2)
                       + jnp.roll(field, -1, 3) + jnp.roll(field, 1, 3) - 4.0 * field)
            field = field + spread_rate * laplace
            rounded = field.astype(jnp.bfloat16).reshape(VL, NXG * NYG)
            tendency = jnp.dot(column_op[section_index], rounded, preferred_element_type=jnp.float32)
            field = field + tendency.reshape(VARS, LEV, NXG, NYG)
        added = jnp.transpose(flux[section_index], (2, 0, 1, 3)).reshape(VARS, NXG, NYG)
        field = field.at[:, 0].add(0.5 * added)
        results.append(field)
    return jnp.stack(results)
```

```python
import jax
import jax.numpy as jnp
from jax import lax
from jax.experimental import pallas as pl
from jax.experimental.pallas import tpu as pltpu
from jax.sharding import PartitionSpec as P

VARS = 8
LEV = 72
VL = VARS * LEV
LANES = 128
TAIL = 16
TOP = 32767.0
AXES = ("sec", "tile", "col")
VMEM = pl.BlockSpec(memory_space=pltpu.VMEM)
SMEM = pl.BlockSpec(memory_space=pltpu.SMEM)
INTERPRET = False


def roll(x, shift):
    return pltpu.roll(x, shift % LANES, x.ndim - 1)


def lane_index(rows):
    return lax.broadcasted_iota(jnp.int32, (rows, LANES), 1)


def encode_kernel(x_ref, msg_ref):
    rows = [x_ref[pl.ds(r, VL, stride=2), :] for r in range(2)]
    top = jnp.max(jnp.maximum(jnp.abs(rows[0]), jnp.abs(rows[1])), axis=0, keepdims=True)
    top = jnp.max(top, axis=1, keepdims=True)
    top = jnp.broadcast_to(jnp.maximum(top, 1e-30), (TAIL, LANES))
    code = jnp.ceil(jnp.log(top) * 64.0)
    scale = (TOP * jnp.exp(code * (-1.0 / 64.0)))[0:1, :]
    for r in range(2):
        q = jnp.clip(jnp.round(rows[r] * scale), -TOP, TOP)
        msg_ref[r * VL : (r + 1) * VL, :] = q.astype(jnp.int32).astype(jnp.int16)
    msg_ref[2 * VL :, :] = code.astype(jnp.int32).astype(jnp.int16)


def step_of(msg_ref):
    code = msg_ref[2 * VL :, :].astype(jnp.int32).astype(jnp.float32)
    return (jnp.exp(code * (1.0 / 64.0)) * (1.0 / TOP))[0:1, :]


def decode(msg_ref, r, step):
    return msg_ref[r * VL : (r + 1) * VL, :].astype(jnp.int32).astype(jnp.float32) * step


def edge_lanes(row, ri, packed, lane):
    for v in range(VARS):
        first = 16 * v + 4 * ri
        moved = roll(row[v * LEV : (v + 1) * LEV, :], first + 2)
        packed = jnp.where((lane >= first) & (lane < first + 4), moved, packed)
    return packed


def own_kernel(x_ref, diff_ref, edge_ref, surf_ref, spread_ref):
    lane = lane_index(LEV)
    packed = jnp.zeros((LEV, LANES), jnp.float32)
    for r in range(2):
        packed = edge_lanes(x_ref[pl.ds(r, VL, stride=2), :], r + 1, packed, lane)
        for v in range(VARS):
            surf_ref[r, v : v + 1, :] = x_ref[2 * LEV * v + r : 2 * LEV * v + r + 1, :]
    edge_ref[...] = packed
    diag = lax.broadcasted_iota(jnp.int32, (LANES, LANES), 0) == lax.broadcasted_iota(
        jnp.int32, (LANES, LANES), 1
    )
    for first in range(0, VL, LANES):
        size = min(LANES, VL - first)
        part = diff_ref[0:1, first : first + size]
        column = jnp.sum(jnp.where(diag[:size, :size], part, 0.0), axis=1, keepdims=True)
        spread_ref[first : first + size, :] = jnp.broadcast_to(column, (size, LANES))


def pack_kernel(up_ref, down_ref, edge_ref, surf_ref, full_ref, send_ref, table_ref):
    lane = lane_index(LEV)
    up_step, down_step = step_of(up_ref), step_of(down_ref)
    packed = edge_lanes(decode(up_ref, 1, up_step), 0, edge_ref[...], lane)
    packed = edge_lanes(decode(down_ref, 0, down_step), 3, packed, lane)
    full_ref[...] = packed
    send_ref[...] = packed.astype(jnp.bfloat16)
    for ref, step, base in ((up_ref, up_step, 0), (down_ref, down_step, 4)):
        for r in range(2):
            rows = []
            for v in range(VARS):
                at = r * VL + v * LEV
                block = ref[at // 16 * 16 : at // 16 * 16 + 16, :].astype(jnp.int32)
                rows.append(block[at % 16 : at % 16 + 1, :])
            block = jnp.concatenate(rows, axis=0).astype(jnp.float32) * step
            table_ref[base + r, :, :] = block.astype(jnp.bfloat16)
    for r in range(2):
        table_ref[2 + r, :, :] = surf_ref[r, :, :].astype(jnp.bfloat16)


def swap_inner(x, place):
    return jnp.where(place == 1, roll(x, -1), jnp.where(place == 2, roll(x, 1), x))


def first_kernel(x_ref, up_ref, down_ref, full_ref, recv_ref, spread_ref, op_ref, out_ref, rhs):
    up_step, down_step = step_of(up_ref), step_of(down_ref)
    lane = lane_index(LEV)
    place = lane % 4
    halo = recv_ref[...].astype(jnp.float32)
    own = full_ref[...]
    spread = jnp.zeros((LEV, LANES), jnp.float32)
    for v in range(VARS):
        spread = jnp.where(lane // 16 == v, spread_ref[v * LEV : (v + 1) * LEV, :], spread)
    beside = jnp.where(place == 1, roll(halo, 1) + roll(own, -1), roll(own, 1) + roll(halo, -1))
    corner = halo + spread * (roll(halo, 4) + roll(halo, -4) + beside - 4.0 * halo)
    corner = swap_inner(corner, place)
    halo = swap_inner(halo, place)

    for v in range(VARS):
        block = slice(v * LEV, (v + 1) * LEV)
        field = [
            decode_block(up_ref, 0, v, up_step),
            decode_block(up_ref, 1, v, up_step),
            x_ref[pl.ds(2 * LEV * v, LEV, stride=2), :],
            x_ref[pl.ds(2 * LEV * v + 1, LEV, stride=2), :],
            decode_block(down_ref, 0, v, down_step),
            decode_block(down_ref, 1, v, down_step),
        ]
        rate = spread_ref[block, :]
        for ri in range(4):
            center = field[ri + 1]
            ends = roll(halo, 126 - 16 * v - 4 * ri)
            left = jnp.where(lane == 0, ends, roll(center, 1))
            right = jnp.where(lane == LANES - 1, ends, roll(center, -1))
            center = center + rate * (field[ri + 2] + field[ri] + right + left - 4.0 * center)
            out_ref[ri, block, :] = center
            rhs[block, ri * LANES : (ri + 1) * LANES] = center.astype(jnp.bfloat16)
        moved = roll(corner, -16 * v)
        out_ref[4, block, :] = moved
        rhs[block, 4 * LANES :] = moved.astype(jnp.bfloat16)
    for ri in range(5):
        out_ref[ri] += jnp.dot(
            op_ref[0], rhs[:, ri * LANES : (ri + 1) * LANES], preferred_element_type=jnp.float32
        )


def decode_block(msg_ref, r, v, step):
    at = r * VL + v * LEV
    low = at // 16 * 16
    block = msg_ref[low : low + 80, :].astype(jnp.int32).astype(jnp.float32)
    return block[at - low : at - low + LEV, :] * step


def second_kernel(
    field_ref, spread_ref, op_ref, weight_ref, near_ref, far_ref, entry_ref, pick_ref, count_ref,
    out_ref, rhs,
):
    lane = lane_index(LEV)
    for v in range(VARS):
        block = slice(v * LEV, (v + 1) * LEV)
        rate = spread_ref[block, :]
        field = [field_ref[ri, block, :] for ri in range(5)]
        for r in range(2):
            ri = r + 1
            center = field[ri]
            ends = roll(field[4], 126 - 4 * ri)
            left = jnp.where(lane == 0, ends, roll(center, 1))
            right = jnp.where(lane == LANES - 1, ends, roll(center, -1))
            center = center + rate * (field[ri + 1] + field[ri - 1] + right + left - 4.0 * center)
            out_ref[pl.ds(2 * LEV * v + r, LEV, stride=2), :] = center
            rhs[block, r * LANES : (r + 1) * LANES] = center.astype(jnp.bfloat16)
    for r in range(2):
        out_ref[pl.ds(r, VL, stride=2), :] += jnp.dot(
            op_ref[0], rhs[:, r * LANES : (r + 1) * LANES], preferred_element_type=jnp.float32
        )
    mine = lax.axis_index("sec")
    last = lax.axis_size("sec") - 1
    for r in range(2):
        flux = jnp.zeros((VARS, LANES), jnp.float32)
        for slot in range(4):
            entry = entry_ref[0, r, 0, slot]
            source = jnp.where(mine == last, entry // 6, mine)
            within = entry % 6
            blocks = jnp.where(
                source == 0,
                near_ref[within],
                far_ref[jnp.where(source == 1, 6, 0) + within],
            )
            contrib = jnp.dot(
                blocks, weight_ref[pick_ref[0, r, 0, slot]], preferred_element_type=jnp.float32
            )
            flux = flux + jnp.where(slot < count_ref[0, r, 0], contrib, 0.0)
        flux = 0.5 * flux
        for v in range(VARS):
            at = 2 * LEV * v + r
            out_ref[at : at + 1, :] = out_ref[at : at + 1, :] + flux[v : v + 1, :]


def call(kernel, outs, specs, scratch=(), flops=0, moved=0):
    return pl.pallas_call(
        kernel,
        out_shape=[jax.ShapeDtypeStruct(shape, dtype) for shape, dtype in outs],
        in_specs=specs,
        out_specs=[VMEM] * len(outs),
        scratch_shapes=list(scratch),
        compiler_params=pltpu.CompilerParams(vmem_limit_bytes=40 * 2**20),
        cost_estimate=pl.CostEstimate(flops=flops, bytes_accessed=moved, transcendentals=0),
        interpret=INTERPRET,
    )


def solution(mesh):
    sections, tiles, cols = (mesh.shape[a] for a in AXES)

    def pairs(move):
        def index(s, t, c):
            return (s * tiles + t % tiles) * cols + c % cols

        return [
            (index(s, t, c), index(*move(s, t, c)))
            for s in range(sections)
            for t in range(tiles)
            for c in range(cols)
        ]

    def shards(state, column_op, diffusion, remap_weights, source_rows, weight_index, counts):
        x = state.reshape(2 * VL, LANES)
        (msg,) = call(encode_kernel, [((2 * VL + TAIL, LANES), jnp.int16)], [VMEM], moved=10**6)(x)
        up = lax.ppermute(msg, AXES, pairs(lambda s, t, c: (s, t + 1, c)))
        down = lax.ppermute(msg, AXES, pairs(lambda s, t, c: (s, t - 1, c)))
        edge, surf, spread = call(
            own_kernel,
            [((LEV, LANES), jnp.float32), ((2, VARS, LANES), jnp.float32), ((VL, LANES), jnp.float32)],
            [VMEM] * 2,
            moved=10**6,
        )(x, diffusion)
        full, send, table = call(
            pack_kernel,
            [((LEV, LANES), jnp.float32), ((LEV, LANES), jnp.bfloat16), ((6, VARS, LANES), jnp.bfloat16)],
            [VMEM] * 4,
            moved=10**6,
        )(up, down, edge, surf)
        near = lax.ppermute(table, AXES, pairs(lambda s, t, c: (3 - s, t, c)))
        recv = lax.ppermute(send, AXES, pairs(lambda s, t, c: (s, t, c + 1)))
        both = jnp.concatenate([table, near], axis=0)
        far = lax.ppermute(both, AXES, pairs(lambda s, t, c: (s ^ 1, t, c)))
        (field,) = call(
            first_kernel,
            [((5, VL, LANES), jnp.float32)],
            [VMEM] * 7,
            [pltpu.VMEM((VL, 5 * LANES), jnp.bfloat16)],
            flops=2 * VL * VL * 5 * LANES,
            moved=2 * 10**6,
        )(x, up, down, full, recv, spread, column_op)
        (out,) = call(
            second_kernel,
            [((2 * VL, LANES), jnp.float32)],
            [VMEM] * 6 + [SMEM] * 3,
            [pltpu.VMEM((VL, 2 * LANES), jnp.bfloat16)],
            flops=2 * VL * VL * 2 * LANES,
            moved=2 * 10**6,
        )(field, spread, column_op, remap_weights, near, far, source_rows, weight_index, counts)
        return out.reshape(1, VARS, LEV, 2, LANES)

    in_specs = (
        P("sec", None, None, "tile", "col"),
        P("sec", None, None),
        P("sec", None),
        P(),
        P("sec", "tile", "col", None),
        P("sec", "tile", "col", None),
        P("sec", "tile", "col"),
    )
    out_specs = P("sec", None, None, "tile", "col")
    return jax.shard_map(shards, mesh=mesh, in_specs=in_specs, out_specs=out_specs, check_vma=False)
```

```python
import jax
import jax.numpy as jnp
from jax import lax
from jax.experimental import pallas as pl
from jax.experimental.pallas import tpu as pltpu
from jax.sharding import PartitionSpec as P

VARS = 8
LEV = 72
VL = VARS * LEV
LANES = 128
TAIL = 16
TOP = 32767.0
AXES = ("sec", "tile", "col")
VMEM = pl.BlockSpec(memory_space=pltpu.VMEM)
HBM = pl.BlockSpec(memory_space=pltpu.HBM)
SMEM = pl.BlockSpec(memory_space=pltpu.SMEM)


def roll(x, shift):
    return pltpu.roll(x, shift % LANES, x.ndim - 1)


def lane_index(rows):
    return lax.broadcasted_iota(jnp.int32, (rows, LANES), 1)


def side():
    return lax.axis_index("tile") % 2


def encode_kernel(x_ref, msg_ref):
    top = jnp.max(jnp.abs(x_ref[...]), axis=0, keepdims=True)
    top = jnp.max(top, axis=1, keepdims=True)
    rows = [x_ref[pl.ds(side(), VL, stride=2), :], x_ref[pl.ds(1 - side(), VL, stride=2), :]]
    top = jnp.broadcast_to(jnp.maximum(top, 1e-30), (TAIL, LANES))
    code = jnp.ceil(jnp.log(top) * 64.0)
    scale = (TOP * jnp.exp(code * (-1.0 / 64.0)))[0:1, :]
    for r in range(2):
        q = jnp.clip(jnp.round(rows[r] * scale), -TOP, TOP)
        msg_ref[r * VL : (r + 1) * VL, :] = q.astype(jnp.int32).astype(jnp.int16)
    msg_ref[2 * VL :, :] = code.astype(jnp.int32).astype(jnp.int16)


def step_of(msg_ref):
    code = msg_ref[2 * VL :, :].astype(jnp.int32).astype(jnp.float32)
    return (jnp.exp(code * (1.0 / 64.0)) * (1.0 / TOP))[0:1, :]


def decode(msg_ref, r, step):
    return msg_ref[r * VL : (r + 1) * VL, :].astype(jnp.int32).astype(jnp.float32) * step


def edge_lanes(row, ri, packed, lane):
    for v in range(VARS):
        first = 16 * v + 4 * ri
        moved = roll(row[v * LEV : (v + 1) * LEV, :], first + 2)
        packed = jnp.where((lane >= first) & (lane < first + 4), moved, packed)
    return packed


def own_kernel(x_ref, diff_ref, edge_ref, surf_ref, spread_ref):
    lane = lane_index(LEV)
    packed = jnp.zeros((LEV, LANES), jnp.float32)
    for r in range(2):
        place = side() if r == 0 else 1 - side()
        packed = edge_lanes(x_ref[pl.ds(place, VL, stride=2), :], r + 1, packed, lane)
        for v in range(VARS):
            surf_ref[r, v : v + 1, :] = x_ref[pl.ds(2 * LEV * v + place, 1), :]
    edge_ref[...] = packed
    diag = lax.broadcasted_iota(jnp.int32, (LANES, LANES), 0) == lax.broadcasted_iota(
        jnp.int32, (LANES, LANES), 1
    )
    for first in range(0, VL, LANES):
        size = min(LANES, VL - first)
        part = diff_ref[0:1, first : first + size]
        column = jnp.sum(jnp.where(diag[:size, :size], part, 0.0), axis=1, keepdims=True)
        spread_ref[first : first + size, :] = jnp.broadcast_to(column, (size, LANES))


def pack_kernel(link_ref, mate_ref, edge_ref, surf_ref, full_ref, send_ref, table_ref):
    lane = lane_index(LEV)
    link_step, mate_step = step_of(link_ref), step_of(mate_ref)
    packed = edge_lanes(decode(link_ref, 0, link_step), 0, edge_ref[...], lane)
    packed = edge_lanes(decode(mate_ref, 1, mate_step), 3, packed, lane)
    full_ref[...] = packed
    send_ref[...] = packed.astype(jnp.bfloat16)
    for r in range(2):
        rows, others = [], []
        for v in range(VARS):
            at = (1 - r) * VL + v * LEV
            low = at // 16 * 16
            block = link_ref[low : low + 16, :].astype(jnp.int32)
            rows.append(block[at - low : at - low + 1, :].astype(jnp.float32) * link_step)
            block = mate_ref[low : low + 16, :].astype(jnp.int32)
            others.append(block[at - low : at - low + 1, :].astype(jnp.float32) * mate_step)
        table_ref[r, :, :] = jnp.concatenate(rows, axis=0).astype(jnp.bfloat16)
        table_ref[2 + r, :, :] = surf_ref[r, :, :].astype(jnp.bfloat16)
        table_ref[4 + r, :, :] = jnp.concatenate(others, axis=0).astype(jnp.bfloat16)


def swap_inner(x, place):
    return jnp.where(place == 1, roll(x, -1), jnp.where(place == 2, roll(x, 1), x))


def first_substep(
    x_ref, link_ref, mate_ref, full_ref, halo, spread_ref, op_ref, out_ref, rhs
):
    link_step, mate_step = step_of(link_ref), step_of(mate_ref)
    lane = lane_index(LEV)
    place = lane % 4
    own = full_ref[...]
    spread = jnp.zeros((LEV, LANES), jnp.float32)
    for v in range(VARS):
        spread = jnp.where(lane // 16 == v, spread_ref[v * LEV : (v + 1) * LEV, :], spread)
    beside = jnp.where(place == 1, roll(halo, 1) + roll(own, -1), roll(own, 1) + roll(halo, -1))
    corner = halo + spread * (roll(halo, 4) + roll(halo, -4) + beside - 4.0 * halo)
    corner = swap_inner(corner, place)
    halo = swap_inner(halo, place)

    for v in range(VARS):
        block = slice(v * LEV, (v + 1) * LEV)
        field = [
            decode_block(link_ref, 1, v, link_step),
            decode_block(link_ref, 0, v, link_step),
            x_ref[pl.ds(2 * LEV * v + side(), LEV, stride=2), :],
            x_ref[pl.ds(2 * LEV * v + 1 - side(), LEV, stride=2), :],
            decode_block(mate_ref, 1, v, mate_step),
            decode_block(mate_ref, 0, v, mate_step),
        ]
        rate = spread_ref[block, :]
        for ri in range(4):
            center = field[ri + 1]
            ends = roll(halo, 126 - 16 * v - 4 * ri)
            left = jnp.where(lane == 0, ends, roll(center, 1))
            right = jnp.where(lane == LANES - 1, ends, roll(center, -1))
            center = center + rate * (field[ri + 2] + field[ri] + right + left - 4.0 * center)
            out_ref[ri, block, :] = center
            rhs[block, ri * LANES : (ri + 1) * LANES] = center.astype(jnp.bfloat16)
        moved = roll(corner, -16 * v)
        out_ref[4, block, :] = moved
        rhs[block, 4 * LANES :] = moved.astype(jnp.bfloat16)
    for ri in range(0, 5, 2):
        width = min(2, 5 - ri)
        tendency = jnp.dot(
            op_ref[0],
            rhs[:, ri * LANES : (ri + width) * LANES],
            preferred_element_type=jnp.float32,
        )
        for k in range(width):
            out_ref[ri + k] += tendency[:, k * LANES : (k + 1) * LANES]


def decode_block(msg_ref, r, v, step):
    at = r * VL + v * LEV
    low = at // 16 * 16
    block = msg_ref[low : low + 80, :].astype(jnp.int32).astype(jnp.float32)
    return block[at - low : at - low + LEV, :] * step


def second_substep(field_ref, spread_ref, op_ref, out_ref, rhs, fluxes, out_hbm, sems):
    lane = lane_index(LEV)
    place = side()
    for v in range(VARS):
        block = slice(v * LEV, (v + 1) * LEV)
        rate = spread_ref[block, :]
        field = [field_ref[ri, block, :] for ri in range(5)]
        for r in range(2):
            ri = r + 1
            center = field[ri]
            ends = roll(field[4], 126 - 4 * ri)
            left = jnp.where(lane == 0, ends, roll(center, 1))
            right = jnp.where(lane == LANES - 1, ends, roll(center, -1))
            center = center + rate * (field[ri + 1] + field[ri - 1] + right + left - 4.0 * center)
            at = 2 * LEV * v + (place if r == 0 else 1 - place)
            out_ref[pl.ds(at, LEV, stride=2), :] = center
            rhs[block, r * LANES : (r + 1) * LANES] = center.astype(jnp.bfloat16)
    half = VL // 2
    copies = []
    for part in range(2):
        tendency = jnp.dot(
            op_ref[0, part * half : (part + 1) * half, :],
            rhs[:, : 2 * LANES],
            preferred_element_type=jnp.float32,
        )
        for r in range(2):
            rows = pl.ds(2 * half * part + (place if r == 0 else 1 - place), half, stride=2)
            out_ref[rows, :] += tendency[:, r * LANES : (r + 1) * LANES]
        for v in range(part * VARS // 2, (part + 1) * VARS // 2):
            for r in range(2):
                at = 2 * LEV * v + r
                out_ref[at : at + 1, :] = out_ref[at : at + 1, :] + fluxes[r][v : v + 1, :]
        rows = pl.ds(part * VL, VL)
        copies.append(pltpu.make_async_copy(out_ref.at[rows, :], out_hbm.at[rows, :], sems.at[part]))
        copies[part].start()
    for copy in copies:
        copy.wait()


def flux_of(weight_ref, near_ref, far_ref, entry_ref, pick_ref, count_ref):
    mine = lax.axis_index("sec")
    place = side()
    fluxes = []
    for r in range(2):
        blocks, weights = [], []
        for slot in range(4):
            entry = entry_ref[0, r, 0, slot]
            apart = mine ^ (entry // 6)
            within = entry % 6
            within = jnp.where(place == 0, within, 5 - within)
            block = jnp.where(
                apart == 2, near_ref[within], far_ref[jnp.where(apart == 3, 6, 0) + within]
            )
            blocks.append(jnp.where(slot < count_ref[0, r, 0], block, jnp.zeros_like(block)))
            weights.append(weight_ref[pick_ref[0, r, 0, slot]])
        fluxes.append(
            0.5
            * jnp.dot(
                jnp.concatenate(blocks, axis=1),
                jnp.concatenate(weights, axis=0),
                preferred_element_type=jnp.float32,
            )
        )
    return fluxes


def first_kernel(
    x_ref, link_ref, mate_ref, full_ref, recv_ref, spread_ref, op_ref, near_rows, rhs
):
    halo = recv_ref[...].astype(jnp.float32)
    first_substep(x_ref, link_ref, mate_ref, full_ref, halo, spread_ref, op_ref, near_rows, rhs)


def second_kernel(
    near_rows, spread_ref, op_ref, weight_ref, near_ref, far_ref, entry_ref, pick_ref, count_ref,
    out_hbm, rhs, out_ref, sems,
):
    fluxes = flux_of(weight_ref, near_ref, far_ref, entry_ref, pick_ref, count_ref)
    second_substep(near_rows, spread_ref, op_ref, out_ref, rhs, fluxes, out_hbm, sems)


def call(kernel, outs, specs, scratch=(), flops=0, moved=0, out_specs=None):
    return pl.pallas_call(
        kernel,
        out_shape=[jax.ShapeDtypeStruct(shape, dtype) for shape, dtype in outs],
        in_specs=specs,
        out_specs=out_specs or [VMEM] * len(outs),
        scratch_shapes=list(scratch),
        compiler_params=pltpu.CompilerParams(vmem_limit_bytes=40 * 2**20),
        cost_estimate=pl.CostEstimate(flops=flops, bytes_accessed=moved, transcendentals=0),
    )


def solution(mesh):
    sections, tiles, cols = (mesh.shape[a] for a in AXES)

    def send(x, move):
        def index(s, t, c):
            return (s * tiles + t) * cols + c

        pairs = [
            (index(s, t, c), index(*move(s, t, c)))
            for s in range(sections)
            for t in range(tiles)
            for c in range(cols)
        ]
        return lax.ppermute(x, AXES, pairs)

    def shards(state, column_op, diffusion, remap_weights, source_rows, weight_index, counts):
        x = state.reshape(2 * VL, LANES)
        wide, narrow = ((LEV, LANES), jnp.float32), ((LEV, LANES), jnp.bfloat16)
        (msg,) = call(encode_kernel, [((2 * VL + TAIL, LANES), jnp.int16)], [VMEM], moved=10**6)(x)
        link = send(msg, lambda s, t, c: (s, (t - 1 + 2 * (t % 2)) % tiles, c))
        mate = send(msg, lambda s, t, c: (s, t + 1 - 2 * (t % 2), c))
        edge, surf, spread = call(
            own_kernel,
            [wide, ((2, VARS, LANES), jnp.float32), ((VL, LANES), jnp.float32)],
            [VMEM] * 2,
            moved=10**6,
        )(x, diffusion)
        full, full16, table = call(
            pack_kernel,
            [wide, narrow, ((6, VARS, LANES), jnp.bfloat16)],
            [VMEM] * 4,
            moved=10**6,
        )(link, mate, edge, surf)
        near = send(table, lambda s, t, c: (s ^ 2, t, c))
        recv = send(full16, lambda s, t, c: (s, t, 1 - c))
        both = jnp.concatenate([table, near], axis=0)
        far = send(both, lambda s, t, c: (s ^ 1, t, c))
        (rows,) = call(
            first_kernel,
            [((5, VL, LANES), jnp.float32)],
            [VMEM] * 7,
            [pltpu.VMEM((VL, 5 * LANES), jnp.bfloat16)],
            flops=2 * VL * VL * 5 * LANES,
            moved=2 * 10**6,
        )(x, link, mate, full, recv, spread, column_op)
        (out,) = call(
            second_kernel,
            [((2 * VL, LANES), jnp.float32)],
            [VMEM] * 6 + [SMEM] * 3,
            [
                pltpu.VMEM((VL, 2 * LANES), jnp.bfloat16),
                pltpu.VMEM((2 * VL, LANES), jnp.float32),
                pltpu.SemaphoreType.DMA((2,)),
            ],
            flops=2 * VL * VL * 2 * LANES,
            moved=2 * 10**6,
            out_specs=[HBM],
        )(rows, spread, column_op, remap_weights, near, far, source_rows, weight_index, counts)
        return out.reshape(1, VARS, LEV, 2, LANES)

    in_specs = (
        P("sec", None, None, "tile", "col"),
        P("sec", None, None),
        P("sec", None),
        P(),
        P("sec", "tile", "col", None),
        P("sec", "tile", "col", None),
        P("sec", "tile", "col"),
    )
    out_specs = P("sec", None, None, "tile", "col")
    return jax.shard_map(shards, mesh=mesh, in_specs=in_specs, out_specs=out_specs, check_vma=False)
```

```python
import jax
import jax.numpy as jnp
from jax import lax
from jax.experimental import pallas as pl
from jax.experimental.pallas import tpu as pltpu
from jax.sharding import PartitionSpec as P

VARS = 8
LEV = 72
VL = VARS * LEV
LANES = 128
TAIL = 16
FOLD = 16
TOP = 32767.0
AXES = ("sec", "tile", "col")
VMEM = pl.BlockSpec(memory_space=pltpu.VMEM)
HBM = pl.BlockSpec(memory_space=pltpu.HBM)
SMEM = pl.BlockSpec(memory_space=pltpu.SMEM)


def roll(x, shift):
    return pltpu.roll(x, shift % LANES, x.ndim - 1)


def lane_index(rows):
    return lax.broadcasted_iota(jnp.int32, (rows, LANES), 1)


def side():
    return lax.axis_index("tile") % 2


def encode_kernel(x_ref, link_ref, mate_ref):
    top = jnp.max(jnp.abs(x_ref[...]), axis=0, keepdims=True)
    top = jnp.max(top, axis=1, keepdims=True)
    rows = [x_ref[pl.ds(side(), VL, stride=2), :], x_ref[pl.ds(1 - side(), VL, stride=2), :]]
    top = jnp.broadcast_to(jnp.maximum(top, 1e-30), (TAIL, LANES))
    code = jnp.ceil(jnp.log(top) * 64.0)
    scale = (TOP * jnp.exp(code * (-1.0 / 64.0)))[0:1, :]
    for r in range(2):
        q = jnp.clip(jnp.round(rows[r] * scale), -TOP, TOP)
        q = q.astype(jnp.int32).astype(jnp.int16)
        link_ref[r * VL : (r + 1) * VL, :] = q
        mate_ref[r * VL : (r + 1) * VL, :] = q
    code = code.astype(jnp.int32).astype(jnp.int16)
    mate_ref[2 * VL :, :] = code
    link_ref[2 * VL : 2 * VL + TAIL, :] = code
    link_ref[2 * VL + TAIL :, :] = code


def step_of(msg_ref):
    code = msg_ref[2 * VL : 2 * VL + TAIL, :].astype(jnp.int32).astype(jnp.float32)
    return (jnp.exp(code * (1.0 / 64.0)) * (1.0 / TOP))[0:1, :]


def decode(msg_ref, r, step):
    return msg_ref[r * VL : (r + 1) * VL, :].astype(jnp.int32).astype(jnp.float32) * step


def edge_lanes(row, ri, packed, lane):
    for v in range(VARS):
        first = 16 * v + 4 * ri
        moved = roll(row[v * LEV : (v + 1) * LEV, :], first + 2)
        packed = jnp.where((lane >= first) & (lane < first + 4), moved, packed)
    return packed


PIECES = (
    ((4, 0), (5, 3), (6, 12), (7, 15)),
    ((8, 0), (9, 3), (10, 12), (11, 15)),
    ((1, 0), (2, 3), (13, 12), (14, 15)),
)


def fold(packed):
    place = lane_index(FOLD) % 16
    kept = LEV - FOLD
    last = packed[kept:, :]
    parts = []
    for i, piece in enumerate(PIECES):
        part = packed[i * FOLD : (i + 1) * FOLD, :]
        for used, free in piece:
            part = jnp.where(place == free, roll(last, free - used), part)
        parts.append(part)
    return jnp.concatenate(parts + [packed[len(PIECES) * FOLD : kept, :]], axis=0)


def unfold(folded):
    place = lane_index(FOLD) % 16
    last = jnp.zeros((FOLD, LANES), jnp.float32)
    for i, piece in enumerate(PIECES):
        part = folded[i * FOLD : (i + 1) * FOLD, :]
        for used, free in piece:
            last = jnp.where(place == used, roll(part, used - free), last)
    return jnp.concatenate([folded, last], axis=0)


def own_kernel(x_ref, diff_ref, edge_ref, surf_ref, spread_ref):
    lane = lane_index(LEV)
    packed = jnp.zeros((LEV, LANES), jnp.float32)
    for r in range(2):
        place = side() if r == 0 else 1 - side()
        packed = edge_lanes(x_ref[pl.ds(place, VL, stride=2), :], r + 1, packed, lane)
        for v in range(VARS):
            surf_ref[r, v : v + 1, :] = x_ref[pl.ds(2 * LEV * v + place, 1), :]
    edge_ref[...] = packed
    diag = lax.broadcasted_iota(jnp.int32, (LANES, LANES), 0) == lax.broadcasted_iota(
        jnp.int32, (LANES, LANES), 1
    )
    for first in range(0, VL, LANES):
        size = min(LANES, VL - first)
        part = diff_ref[0:1, first : first + size]
        column = jnp.sum(jnp.where(diag[:size, :size], part, 0.0), axis=1, keepdims=True)
        spread_ref[first : first + size, :] = jnp.broadcast_to(column, (size, LANES))


def pack_kernel(link_ref, mate_ref, edge_ref, surf_ref, full_ref, send_ref, table_ref):
    lane = lane_index(LEV)
    link_step, mate_step = step_of(link_ref), step_of(mate_ref)
    packed = edge_lanes(decode(link_ref, 0, link_step), 0, edge_ref[...], lane)
    packed = edge_lanes(decode(mate_ref, 1, mate_step), 3, packed, lane)
    full_ref[...] = packed
    send_ref[...] = fold(packed).astype(jnp.bfloat16)
    for r in range(2):
        rows, others = [], []
        for v in range(VARS):
            at = (1 - r) * VL + v * LEV
            low = at // 16 * 16
            block = link_ref[low : low + 16, :].astype(jnp.int32)
            rows.append(block[at - low : at - low + 1, :].astype(jnp.float32) * link_step)
            block = mate_ref[low : low + 16, :].astype(jnp.int32)
            others.append(block[at - low : at - low + 1, :].astype(jnp.float32) * mate_step)
        table_ref[r, :, :] = jnp.concatenate(rows, axis=0).astype(jnp.bfloat16)
        table_ref[2 + r, :, :] = surf_ref[r, :, :].astype(jnp.bfloat16)
        table_ref[4 + r, :, :] = jnp.concatenate(others, axis=0).astype(jnp.bfloat16)


def swap_inner(x, place):
    return jnp.where(place == 1, roll(x, -1), jnp.where(place == 2, roll(x, 1), x))


def interior_kernel(x_ref, link_ref, mate_ref, spread_ref, near_ref, rows_ref, rate_ref):
    del near_ref
    link_step, mate_step = step_of(link_ref), step_of(mate_ref)
    lane = lane_index(LEV)
    rates = jnp.zeros((LEV, LANES), jnp.float32)
    for v in range(VARS):
        rates = jnp.where(lane // 16 == v, spread_ref[v * LEV : (v + 1) * LEV, :], rates)
    rate_ref[...] = rates
    for v in range(VARS):
        block = slice(v * LEV, (v + 1) * LEV)
        field = [
            decode_block(link_ref, 1, v, link_step),
            decode_block(link_ref, 0, v, link_step),
            x_ref[pl.ds(2 * LEV * v + side(), LEV, stride=2), :],
            x_ref[pl.ds(2 * LEV * v + 1 - side(), LEV, stride=2), :],
            decode_block(mate_ref, 1, v, mate_step),
            decode_block(mate_ref, 0, v, mate_step),
        ]
        rate = spread_ref[block, :]
        for ri in range(4):
            center = field[ri + 1]
            left = jnp.where(lane == 0, 0.0, roll(center, 1))
            right = jnp.where(lane == LANES - 1, 0.0, roll(center, -1))
            rows_ref[ri, block, :] = center + rate * (
                field[ri + 2] + field[ri] + right + left - 4.0 * center
            )


def first_kernel(rows_ref, full_ref, recv_ref, rate_ref, op_ref, out_ref, rhs):
    lane = lane_index(LEV)
    place = lane % 4
    halo = unfold(recv_ref[...].astype(jnp.float32))
    own = full_ref[...]
    beside = jnp.where(place == 1, roll(halo, 1) + roll(own, -1), roll(own, 1) + roll(halo, -1))
    corner = halo + rate_ref[...] * (roll(halo, 4) + roll(halo, -4) + beside - 4.0 * halo)
    corner = swap_inner(corner, place)
    halo = swap_inner(halo * rate_ref[...], place)
    ends = (lane == 0) | (lane == LANES - 1)
    for v in range(VARS):
        block = slice(v * LEV, (v + 1) * LEV)
        for ri in range(4):
            beyond = jnp.where(ends, roll(halo, 126 - 16 * v - 4 * ri), 0.0)
            center = rows_ref[ri, block, :] + beyond
            out_ref[ri, block, :] = center
            rhs[block, ri * LANES : (ri + 1) * LANES] = center.astype(jnp.bfloat16)
        moved = roll(corner, -16 * v)
        out_ref[4, block, :] = moved
        rhs[block, 4 * LANES :] = moved.astype(jnp.bfloat16)
    for ri in range(0, 5, 2):
        width = min(2, 5 - ri)
        tendency = jnp.dot(
            op_ref[0],
            rhs[:, ri * LANES : (ri + width) * LANES],
            preferred_element_type=jnp.float32,
        )
        for k in range(width):
            out_ref[ri + k] += tendency[:, k * LANES : (k + 1) * LANES]


def decode_block(msg_ref, r, v, step):
    at = r * VL + v * LEV
    low = at // 16 * 16
    block = msg_ref[low : low + 80, :].astype(jnp.int32).astype(jnp.float32)
    return block[at - low : at - low + LEV, :] * step


def second_kernel(
    field_ref, spread_ref, op_ref, weight_ref, near_ref, far_ref, entry_ref, pick_ref, count_ref,
    out_hbm, rhs, out_ref, sems,
):
    lane = lane_index(LEV)
    fluxes = [
        flux_of(r, weight_ref, near_ref, far_ref, entry_ref, pick_ref, count_ref) for r in range(2)
    ]
    place = side()
    for v in range(VARS):
        block = slice(v * LEV, (v + 1) * LEV)
        rate = spread_ref[block, :]
        field = [field_ref[ri, block, :] for ri in range(5)]
        for r in range(2):
            ri = r + 1
            center = field[ri]
            ends = roll(field[4], 126 - 4 * ri)
            left = jnp.where(lane == 0, ends, roll(center, 1))
            right = jnp.where(lane == LANES - 1, ends, roll(center, -1))
            center = center + rate * (field[ri + 1] + field[ri - 1] + right + left - 4.0 * center)
            at = 2 * LEV * v + (place if r == 0 else 1 - place)
            out_ref[pl.ds(at, LEV, stride=2), :] = center
            rhs[block, r * LANES : (r + 1) * LANES] = center.astype(jnp.bfloat16)
    half = VL // 2
    copies = []
    for part in range(2):
        tendency = jnp.dot(
            op_ref[0, part * half : (part + 1) * half, :],
            rhs[:, : 2 * LANES],
            preferred_element_type=jnp.float32,
        )
        for r in range(2):
            rows = pl.ds(2 * half * part + (place if r == 0 else 1 - place), half, stride=2)
            out_ref[rows, :] += tendency[:, r * LANES : (r + 1) * LANES]
        for v in range(part * VARS // 2, (part + 1) * VARS // 2):
            for r in range(2):
                at = 2 * LEV * v + r
                out_ref[at : at + 1, :] = out_ref[at : at + 1, :] + fluxes[r][v : v + 1, :]
        rows = pl.ds(part * VL, VL)
        copies.append(pltpu.make_async_copy(out_ref.at[rows, :], out_hbm.at[rows, :], sems.at[part]))
        copies[part].start()
    for copy in copies:
        copy.wait()


def flux_of(r, weight_ref, near_ref, far_ref, entry_ref, pick_ref, count_ref):
    mine = lax.axis_index("sec")
    blocks, weights = [], []
    for slot in range(4):
        entry = entry_ref[0, r, 0, slot]
        apart = mine ^ (entry // 6)
        within = entry % 6
        within = jnp.where(side() == 0, within, 5 - within)
        block = jnp.where(
            apart == 2, near_ref[within], far_ref[jnp.where(apart == 3, 6, 0) + within]
        )
        blocks.append(jnp.where(slot < count_ref[0, r, 0], block, jnp.zeros_like(block)))
        weights.append(weight_ref[pick_ref[0, r, 0, slot]])
    blocks, weights = jnp.concatenate(blocks, axis=1), jnp.concatenate(weights, axis=0)
    return 0.5 * jnp.dot(blocks, weights, preferred_element_type=jnp.float32)


def call(kernel, outs, specs, scratch=(), flops=0, moved=0, out_specs=None):
    return pl.pallas_call(
        kernel,
        out_shape=[jax.ShapeDtypeStruct(shape, dtype) for shape, dtype in outs],
        in_specs=specs,
        out_specs=out_specs or [VMEM] * len(outs),
        scratch_shapes=list(scratch),
        compiler_params=pltpu.CompilerParams(vmem_limit_bytes=40 * 2**20),
        cost_estimate=pl.CostEstimate(flops=flops, bytes_accessed=moved, transcendentals=0),
    )


def solution(mesh):
    sections, tiles, cols = (mesh.shape[a] for a in AXES)

    def send(x, move):
        def index(s, t, c):
            return (s * tiles + t) * cols + c

        pairs = [
            (index(s, t, c), index(*move(s, t, c)))
            for s in range(sections)
            for t in range(tiles)
            for c in range(cols)
        ]
        return lax.ppermute(x, AXES, pairs)

    def shards(state, column_op, diffusion, remap_weights, source_rows, weight_index, counts):
        x = state.reshape(2 * VL, LANES)
        wide, narrow = ((LEV, LANES), jnp.float32), ((LEV - FOLD, LANES), jnp.bfloat16)
        to_link, to_mate = call(
            encode_kernel,
            [((2 * VL + 2 * TAIL, LANES), jnp.int16), ((2 * VL + TAIL, LANES), jnp.int16)],
            [VMEM],
            moved=10**6,
        )(x)
        link = send(to_link, lambda s, t, c: (s, (t - 1 + 2 * (t % 2)) % tiles, c))
        mate = send(to_mate, lambda s, t, c: (s, t + 1 - 2 * (t % 2), c))
        edge, surf, spread = call(
            own_kernel,
            [wide, ((2, VARS, LANES), jnp.float32), ((VL, LANES), jnp.float32)],
            [VMEM] * 2,
            moved=10**6,
        )(x, diffusion)
        full, full16, table = call(
            pack_kernel,
            [wide, narrow, ((6, VARS, LANES), jnp.bfloat16)],
            [VMEM] * 4,
            moved=10**6,
        )(link, mate, edge, surf)
        near = send(table, lambda s, t, c: (s ^ 2, t, c))
        recv = send(full16, lambda s, t, c: (s, t, 1 - c))
        both = jnp.concatenate([table, near], axis=0)
        far = send(both, lambda s, t, c: (s ^ 1, t, c))
        inner, rates = call(
            interior_kernel,
            [((4, VL, LANES), jnp.float32), wide],
            [VMEM] * 5,
            moved=3 * 10**6,
        )(x, link, mate, spread, near)
        (rows,) = call(
            first_kernel,
            [((5, VL, LANES), jnp.float32)],
            [VMEM] * 5,
            [pltpu.VMEM((VL, 5 * LANES), jnp.bfloat16)],
            flops=2 * VL * VL * 5 * LANES,
            moved=2 * 10**6,
        )(inner, full, recv, rates, column_op)
        (out,) = call(
            second_kernel,
            [((2 * VL, LANES), jnp.float32)],
            [VMEM] * 6 + [SMEM] * 3,
            [
                pltpu.VMEM((VL, 2 * LANES), jnp.bfloat16),
                pltpu.VMEM((2 * VL, LANES), jnp.float32),
                pltpu.SemaphoreType.DMA((2,)),
            ],
            flops=2 * VL * VL * 2 * LANES,
            moved=2 * 10**6,
            out_specs=[HBM],
        )(rows, spread, column_op, remap_weights, near, far, source_rows, weight_index, counts)
        return out.reshape(1, VARS, LEV, 2, LANES)

    in_specs = (
        P("sec", None, None, "tile", "col"),
        P("sec", None, None),
        P("sec", None),
        P(),
        P("sec", "tile", "col", None),
        P("sec", "tile", "col", None),
        P("sec", "tile", "col"),
    )
    out_specs = P("sec", None, None, "tile", "col")
    return jax.shard_map(shards, mesh=mesh, in_specs=in_specs, out_specs=out_specs, check_vma=False)
```

```python
import jax
import jax.numpy as jnp
from jax import lax
from jax.experimental import pallas as pl
from jax.experimental.pallas import tpu as pltpu
from jax.sharding import PartitionSpec as P

VARS = 8
LEV = 72
VL = VARS * LEV
LANES = 128
TAIL = 16
FOLD = 16
PARTS = ((0, 4), (4, 6), (6, 8))
TOP = 32767.0
AXES = ("sec", "tile", "col")
VMEM = pl.BlockSpec(memory_space=pltpu.VMEM)
HBM = pl.BlockSpec(memory_space=pltpu.HBM)
SMEM = pl.BlockSpec(memory_space=pltpu.SMEM)


def roll(x, shift):
    return pltpu.roll(x, shift % LANES, x.ndim - 1)


def lane_index(rows):
    return lax.broadcasted_iota(jnp.int32, (rows, LANES), 1)


def side():
    return lax.axis_index("tile") % 2


def encode_kernel(x_ref, link_ref, mate_ref):
    top = jnp.max(jnp.abs(x_ref[...]), axis=0, keepdims=True)
    top = jnp.max(top, axis=1, keepdims=True)
    rows = [x_ref[pl.ds(side(), VL, stride=2), :], x_ref[pl.ds(1 - side(), VL, stride=2), :]]
    top = jnp.broadcast_to(jnp.maximum(top, 1e-30), (TAIL, LANES))
    code = jnp.ceil(jnp.log(top) * 64.0)
    scale = (TOP * jnp.exp(code * (-1.0 / 64.0)))[0:1, :]
    for r in range(2):
        q = jnp.clip(jnp.round(rows[r] * scale), -TOP, TOP)
        q = q.astype(jnp.int32).astype(jnp.int16)
        link_ref[r * VL : (r + 1) * VL, :] = q
        mate_ref[r * VL : (r + 1) * VL, :] = q
    code = code.astype(jnp.int32).astype(jnp.int16)
    mate_ref[2 * VL :, :] = code
    link_ref[2 * VL : 2 * VL + TAIL, :] = code
    link_ref[2 * VL + TAIL :, :] = code


def step_of(msg_ref):
    code = msg_ref[2 * VL : 2 * VL + TAIL, :].astype(jnp.int32).astype(jnp.float32)
    return (jnp.exp(code * (1.0 / 64.0)) * (1.0 / TOP))[0:1, :]


def decode(msg_ref, r, step):
    return msg_ref[r * VL : (r + 1) * VL, :].astype(jnp.int32).astype(jnp.float32) * step


def edge_lanes(row, ri, packed, lane):
    for v in range(VARS):
        first = 16 * v + 4 * ri
        moved = roll(row[v * LEV : (v + 1) * LEV, :], first + 2)
        packed = jnp.where((lane >= first) & (lane < first + 4), moved, packed)
    return packed


PIECES = (
    ((4, 0), (5, 3), (6, 12), (7, 15)),
    ((8, 0), (9, 3), (10, 12), (11, 15)),
    ((1, 0), (2, 3), (13, 12), (14, 15)),
)


def fold(packed):
    place = lane_index(FOLD) % 16
    kept = LEV - FOLD
    last = packed[kept:, :]
    parts = []
    for i, piece in enumerate(PIECES):
        part = packed[i * FOLD : (i + 1) * FOLD, :]
        for used, free in piece:
            part = jnp.where(place == free, roll(last, free - used), part)
        parts.append(part)
    return jnp.concatenate(parts + [packed[len(PIECES) * FOLD : kept, :]], axis=0)


def unfold(folded):
    place = lane_index(FOLD) % 16
    last = jnp.zeros((FOLD, LANES), jnp.float32)
    for i, piece in enumerate(PIECES):
        part = folded[i * FOLD : (i + 1) * FOLD, :]
        for used, free in piece:
            last = jnp.where(place == used, roll(part, used - free), last)
    return jnp.concatenate([folded, last], axis=0)


def own_kernel(x_ref, diff_ref, edge_ref, surf_ref, spread_ref):
    lane = lane_index(LEV)
    packed = jnp.zeros((LEV, LANES), jnp.float32)
    for r in range(2):
        place = side() if r == 0 else 1 - side()
        packed = edge_lanes(x_ref[pl.ds(place, VL, stride=2), :], r + 1, packed, lane)
        for v in range(VARS):
            surf_ref[r, v : v + 1, :] = x_ref[pl.ds(2 * LEV * v + place, 1), :]
    edge_ref[...] = packed
    diag = lax.broadcasted_iota(jnp.int32, (LANES, LANES), 0) == lax.broadcasted_iota(
        jnp.int32, (LANES, LANES), 1
    )
    for first in range(0, VL, LANES):
        size = min(LANES, VL - first)
        part = diff_ref[0:1, first : first + size]
        column = jnp.sum(jnp.where(diag[:size, :size], part, 0.0), axis=1, keepdims=True)
        spread_ref[first : first + size, :] = jnp.broadcast_to(column, (size, LANES))


def pack_kernel(link_ref, mate_ref, edge_ref, surf_ref, full_ref, send_ref, table_ref):
    lane = lane_index(LEV)
    link_step, mate_step = step_of(link_ref), step_of(mate_ref)
    packed = edge_lanes(decode(link_ref, 0, link_step), 0, edge_ref[...], lane)
    packed = edge_lanes(decode(mate_ref, 1, mate_step), 3, packed, lane)
    full_ref[...] = packed
    send_ref[...] = fold(packed).astype(jnp.bfloat16)
    for r in range(2):
        rows, others = [], []
        for v in range(VARS):
            at = (1 - r) * VL + v * LEV
            low = at // 16 * 16
            block = link_ref[low : low + 16, :].astype(jnp.int32)
            rows.append(block[at - low : at - low + 1, :].astype(jnp.float32) * link_step)
            block = mate_ref[low : low + 16, :].astype(jnp.int32)
            others.append(block[at - low : at - low + 1, :].astype(jnp.float32) * mate_step)
        table_ref[r, :, :] = jnp.concatenate(rows, axis=0).astype(jnp.bfloat16)
        table_ref[2 + r, :, :] = surf_ref[r, :, :].astype(jnp.bfloat16)
        table_ref[4 + r, :, :] = jnp.concatenate(others, axis=0).astype(jnp.bfloat16)


def swap_inner(x, place):
    return jnp.where(place == 1, roll(x, -1), jnp.where(place == 2, roll(x, 1), x))


def interior_kernel(x_ref, link_ref, mate_ref, spread_ref, near_ref, rows_ref, rate_ref):
    del near_ref
    link_step, mate_step = step_of(link_ref), step_of(mate_ref)
    lane = lane_index(LEV)
    rates = jnp.zeros((LEV, LANES), jnp.float32)
    for v in range(VARS):
        rates = jnp.where(lane // 16 == v, spread_ref[v * LEV : (v + 1) * LEV, :], rates)
    rate_ref[...] = rates
    for v in range(VARS):
        block = slice(v * LEV, (v + 1) * LEV)
        field = [
            decode_block(link_ref, 1, v, link_step),
            decode_block(link_ref, 0, v, link_step),
            x_ref[pl.ds(2 * LEV * v + side(), LEV, stride=2), :],
            x_ref[pl.ds(2 * LEV * v + 1 - side(), LEV, stride=2), :],
            decode_block(mate_ref, 1, v, mate_step),
            decode_block(mate_ref, 0, v, mate_step),
        ]
        rate = spread_ref[block, :]
        for ri in range(4):
            center = field[ri + 1]
            left = jnp.where(lane == 0, 0.0, roll(center, 1))
            right = jnp.where(lane == LANES - 1, 0.0, roll(center, -1))
            rows_ref[ri, block, :] = center + rate * (
                field[ri + 2] + field[ri] + right + left - 4.0 * center
            )


def first_kernel(
    rows_ref, full_ref, recv_ref, rate_ref, spread_ref, op_ref, center_ref, rounded_ref, rhs, out_ref
):
    lane = lane_index(LEV)
    place = lane % 4
    halo = unfold(recv_ref[...].astype(jnp.float32))
    own = full_ref[...]
    beside = jnp.where(place == 1, roll(halo, 1) + roll(own, -1), roll(own, 1) + roll(halo, -1))
    corner = halo + rate_ref[...] * (roll(halo, 4) + roll(halo, -4) + beside - 4.0 * halo)
    corner = swap_inner(corner, place)
    halo = swap_inner(halo * rate_ref[...], place)
    ends = (lane == 0) | (lane == LANES - 1)
    for v in range(VARS):
        block = slice(v * LEV, (v + 1) * LEV)
        for ri in range(4):
            beyond = jnp.where(ends, roll(halo, 126 - 16 * v - 4 * ri), 0.0)
            center = rows_ref[ri, block, :] + beyond
            out_ref[ri, block, :] = center
            rhs[block, ri * LANES : (ri + 1) * LANES] = center.astype(jnp.bfloat16)
        moved = roll(corner, -16 * v)
        out_ref[4, block, :] = moved
        rhs[block, 4 * LANES :] = moved.astype(jnp.bfloat16)
    for ri in range(0, 5, 2):
        width = min(2, 5 - ri)
        tendency = jnp.dot(
            op_ref[0],
            rhs[:, ri * LANES : (ri + width) * LANES],
            preferred_element_type=jnp.float32,
        )
        for k in range(width):
            out_ref[ri + k] += tendency[:, k * LANES : (k + 1) * LANES]
    second_stencil(out_ref, spread_ref, center_ref, rounded_ref)


def decode_block(msg_ref, r, v, step):
    at = r * VL + v * LEV
    low = at // 16 * 16
    block = msg_ref[low : low + 80, :].astype(jnp.int32).astype(jnp.float32)
    return block[at - low : at - low + LEV, :] * step


def second_stencil(field_ref, spread_ref, center_ref, rounded_ref):
    lane = lane_index(LEV)
    place = side()
    for v in range(VARS):
        block = slice(v * LEV, (v + 1) * LEV)
        rate = spread_ref[block, :]
        field = [field_ref[ri, block, :] for ri in range(5)]
        for r in range(2):
            ri = r + 1
            center = field[ri]
            ends = roll(field[4], 126 - 4 * ri)
            left = jnp.where(lane == 0, ends, roll(center, 1))
            right = jnp.where(lane == LANES - 1, ends, roll(center, -1))
            center = center + rate * (field[ri + 1] + field[ri - 1] + right + left - 4.0 * center)
            at = 2 * LEV * v + (place if r == 0 else 1 - place)
            center_ref[pl.ds(at, LEV, stride=2), :] = center
            rounded_ref[block, r * LANES : (r + 1) * LANES] = center.astype(jnp.bfloat16)


def second_kernel(
    center_ref, rounded_ref, op_ref, weight_ref, near_ref, far_ref, entry_ref, pick_ref, count_ref,
    out_hbm, out_ref, sems,
):
    fluxes = [
        flux_of(r, weight_ref, near_ref, far_ref, entry_ref, pick_ref, count_ref) for r in range(2)
    ]
    place = side()
    copies = []
    for i, (low, high) in enumerate(PARTS):
        size = (high - low) * LEV
        tendency = jnp.dot(
            op_ref[0, low * LEV : high * LEV, :],
            rounded_ref[...],
            preferred_element_type=jnp.float32,
        )
        for r in range(2):
            rows = pl.ds(2 * LEV * low + (place if r == 0 else 1 - place), size, stride=2)
            out_ref[rows, :] = center_ref[rows, :] + tendency[:, r * LANES : (r + 1) * LANES]
        for v in range(low, high):
            for r in range(2):
                at = 2 * LEV * v + r
                out_ref[at : at + 1, :] = out_ref[at : at + 1, :] + fluxes[r][v : v + 1, :]
        rows = pl.ds(2 * LEV * low, 2 * size)
        copies.append(pltpu.make_async_copy(out_ref.at[rows, :], out_hbm.at[rows, :], sems.at[i]))
        copies[i].start()
    for copy in copies:
        copy.wait()


def flux_of(r, weight_ref, near_ref, far_ref, entry_ref, pick_ref, count_ref):
    mine = lax.axis_index("sec")
    blocks, weights = [], []
    for slot in range(4):
        entry = entry_ref[0, r, 0, slot]
        apart = mine ^ (entry // 6)
        within = entry % 6
        within = jnp.where(side() == 0, within, 5 - within)
        block = jnp.where(
            apart == 2, near_ref[within], far_ref[jnp.where(apart == 3, 6, 0) + within]
        )
        blocks.append(jnp.where(slot < count_ref[0, r, 0], block, jnp.zeros_like(block)))
        weights.append(weight_ref[pick_ref[0, r, 0, slot]])
    blocks, weights = jnp.concatenate(blocks, axis=1), jnp.concatenate(weights, axis=0)
    return 0.5 * jnp.dot(blocks, weights, preferred_element_type=jnp.float32)


def call(kernel, outs, specs, scratch=(), flops=0, moved=0, out_specs=None):
    return pl.pallas_call(
        kernel,
        out_shape=[jax.ShapeDtypeStruct(shape, dtype) for shape, dtype in outs],
        in_specs=specs,
        out_specs=out_specs or [VMEM] * len(outs),
        scratch_shapes=list(scratch),
        compiler_params=pltpu.CompilerParams(vmem_limit_bytes=40 * 2**20),
        cost_estimate=pl.CostEstimate(flops=flops, bytes_accessed=moved, transcendentals=0),
    )


def solution(mesh):
    sections, tiles, cols = (mesh.shape[a] for a in AXES)

    def send(x, move):
        def index(s, t, c):
            return (s * tiles + t) * cols + c

        pairs = [
            (index(s, t, c), index(*move(s, t, c)))
            for s in range(sections)
            for t in range(tiles)
            for c in range(cols)
        ]
        return lax.ppermute(x, AXES, pairs)

    def shards(state, column_op, diffusion, remap_weights, source_rows, weight_index, counts):
        x = state.reshape(2 * VL, LANES)
        wide, narrow = ((LEV, LANES), jnp.float32), ((LEV - FOLD, LANES), jnp.bfloat16)
        to_link, to_mate = call(
            encode_kernel,
            [((2 * VL + 2 * TAIL, LANES), jnp.int16), ((2 * VL + TAIL, LANES), jnp.int16)],
            [VMEM],
            moved=10**6,
        )(x)
        link = send(to_link, lambda s, t, c: (s, (t - 1 + 2 * (t % 2)) % tiles, c))
        mate = send(to_mate, lambda s, t, c: (s, t + 1 - 2 * (t % 2), c))
        edge, surf, spread = call(
            own_kernel,
            [wide, ((2, VARS, LANES), jnp.float32), ((VL, LANES), jnp.float32)],
            [VMEM] * 2,
            moved=10**6,
        )(x, diffusion)
        full, full16, table = call(
            pack_kernel,
            [wide, narrow, ((6, VARS, LANES), jnp.bfloat16)],
            [VMEM] * 4,
            moved=10**6,
        )(link, mate, edge, surf)
        near = send(table, lambda s, t, c: (s ^ 2, t, c))
        recv = send(full16, lambda s, t, c: (s, t, 1 - c))
        both = jnp.concatenate([table, near], axis=0)
        far = send(both, lambda s, t, c: (s ^ 1, t, c))
        inner, rates = call(
            interior_kernel,
            [((4, VL, LANES), jnp.float32), wide],
            [VMEM] * 5,
            moved=3 * 10**6,
        )(x, link, mate, spread, near)
        center, rounded = call(
            first_kernel,
            [((2 * VL, LANES), jnp.float32), ((VL, 2 * LANES), jnp.bfloat16)],
            [VMEM] * 6,
            [
                pltpu.VMEM((VL, 5 * LANES), jnp.bfloat16),
                pltpu.VMEM((5, VL, LANES), jnp.float32),
            ],
            flops=2 * VL * VL * 5 * LANES,
            moved=2 * 10**6,
        )(inner, full, recv, rates, spread, column_op)
        (out,) = call(
            second_kernel,
            [((2 * VL, LANES), jnp.float32)],
            [VMEM] * 6 + [SMEM] * 3,
            [
                pltpu.VMEM((2 * VL, LANES), jnp.float32),
                pltpu.SemaphoreType.DMA((len(PARTS),)),
            ],
            flops=2 * VL * VL * 2 * LANES,
            moved=2 * 10**6,
            out_specs=[HBM],
        )(center, rounded, column_op, remap_weights, near, far, source_rows, weight_index, counts)
        return out.reshape(1, VARS, LEV, 2, LANES)

    in_specs = (
        P("sec", None, None, "tile", "col"),
        P("sec", None, None),
        P("sec", None),
        P(),
        P("sec", "tile", "col", None),
        P("sec", "tile", "col", None),
        P("sec", "tile", "col"),
    )
    out_specs = P("sec", None, None, "tile", "col")
    return jax.shard_map(shards, mesh=mesh, in_specs=in_specs, out_specs=out_specs, check_vma=False)
```

```python
import jax
import jax.numpy as jnp
from jax import lax
from jax.experimental import pallas as pl
from jax.experimental.pallas import tpu as pltpu
from jax.sharding import PartitionSpec as P

VARS = 8
LEV = 72
VL = VARS * LEV
LANES = 128
TAIL = 16
FOLD = 16
PARTS = ((0, 4), (4, 6), (6, 8))
TOP = 32767.0
AXES = ("sec", "tile", "col")
VMEM = pl.BlockSpec(memory_space=pltpu.VMEM)
HBM = pl.BlockSpec(memory_space=pltpu.HBM)
SMEM = pl.BlockSpec(memory_space=pltpu.SMEM)


def roll(x, shift):
    return pltpu.roll(x, shift % LANES, x.ndim - 1)


def lane_index(rows):
    return lax.broadcasted_iota(jnp.int32, (rows, LANES), 1)


def side():
    return lax.axis_index("tile") % 2


def encode_kernel(x_ref, link_ref, mate_ref):
    top = jnp.max(jnp.abs(x_ref[...]), axis=0, keepdims=True)
    top = jnp.max(top, axis=1, keepdims=True)
    rows = [x_ref[pl.ds(side(), VL, stride=2), :], x_ref[pl.ds(1 - side(), VL, stride=2), :]]
    top = jnp.broadcast_to(jnp.maximum(top, 1e-30), (TAIL, LANES))
    code = jnp.ceil(jnp.log(top) * 64.0)
    scale = (TOP * jnp.exp(code * (-1.0 / 64.0)))[0:1, :]
    for r in range(2):
        q = jnp.clip(jnp.round(rows[r] * scale), -TOP, TOP)
        q = q.astype(jnp.int32).astype(jnp.int16)
        link_ref[r * VL : (r + 1) * VL, :] = q
        mate_ref[r * VL : (r + 1) * VL, :] = q
    code = code.astype(jnp.int32).astype(jnp.int16)
    mate_ref[2 * VL :, :] = code
    link_ref[2 * VL : 2 * VL + TAIL, :] = code
    link_ref[2 * VL + TAIL :, :] = code


def step_of(msg_ref):
    code = msg_ref[2 * VL : 2 * VL + TAIL, :].astype(jnp.int32).astype(jnp.float32)
    return (jnp.exp(code * (1.0 / 64.0)) * (1.0 / TOP))[0:1, :]


def decode(msg_ref, r, step):
    return msg_ref[r * VL : (r + 1) * VL, :].astype(jnp.int32).astype(jnp.float32) * step


def edge_lanes(row, ri, packed, lane):
    for v in range(VARS):
        first = 16 * v + 4 * ri
        moved = roll(row[v * LEV : (v + 1) * LEV, :], first + 2)
        packed = jnp.where((lane >= first) & (lane < first + 4), moved, packed)
    return packed


PIECES = (
    ((4, 0), (5, 3), (6, 12), (7, 15)),
    ((8, 0), (9, 3), (10, 12), (11, 15)),
    ((1, 0), (2, 3), (13, 12), (14, 15)),
)


def fold(packed):
    place = lane_index(FOLD) % 16
    kept = LEV - FOLD
    last = packed[kept:, :]
    parts = []
    for i, piece in enumerate(PIECES):
        part = packed[i * FOLD : (i + 1) * FOLD, :]
        for used, free in piece:
            part = jnp.where(place == free, roll(last, free - used), part)
        parts.append(part)
    return jnp.concatenate(parts + [packed[len(PIECES) * FOLD : kept, :]], axis=0)


def unfold(folded):
    place = lane_index(FOLD) % 16
    last = jnp.zeros((FOLD, LANES), jnp.float32)
    for i, piece in enumerate(PIECES):
        part = folded[i * FOLD : (i + 1) * FOLD, :]
        for used, free in piece:
            last = jnp.where(place == used, roll(part, used - free), last)
    return jnp.concatenate([folded, last], axis=0)


def own_kernel(x_ref, diff_ref, edge_ref, surf_ref, spread_ref):
    lane = lane_index(LEV)
    packed = jnp.zeros((LEV, LANES), jnp.float32)
    for r in range(2):
        place = side() if r == 0 else 1 - side()
        packed = edge_lanes(x_ref[pl.ds(place, VL, stride=2), :], r + 1, packed, lane)
        for v in range(VARS):
            surf_ref[r, v : v + 1, :] = x_ref[pl.ds(2 * LEV * v + place, 1), :]
    edge_ref[...] = packed
    diag = lax.broadcasted_iota(jnp.int32, (LANES, LANES), 0) == lax.broadcasted_iota(
        jnp.int32, (LANES, LANES), 1
    )
    for first in range(0, VL, LANES):
        size = min(LANES, VL - first)
        part = diff_ref[0:1, first : first + size]
        column = jnp.sum(jnp.where(diag[:size, :size], part, 0.0), axis=1, keepdims=True)
        spread_ref[first : first + size, :] = jnp.broadcast_to(column, (size, LANES))


def pack_kernel(link_ref, mate_ref, edge_ref, surf_ref, full_ref, send_ref, table_ref):
    lane = lane_index(LEV)
    link_step, mate_step = step_of(link_ref), step_of(mate_ref)
    packed = edge_lanes(decode(link_ref, 0, link_step), 0, edge_ref[...], lane)
    packed = edge_lanes(decode(mate_ref, 1, mate_step), 3, packed, lane)
    full_ref[...] = packed
    send_ref[...] = fold(packed).astype(jnp.bfloat16)
    for r in range(2):
        rows, others = [], []
        for v in range(VARS):
            at = (1 - r) * VL + v * LEV
            low = at // 16 * 16
            block = link_ref[low : low + 16, :].astype(jnp.int32)
            rows.append(block[at - low : at - low + 1, :].astype(jnp.float32) * link_step)
            block = mate_ref[low : low + 16, :].astype(jnp.int32)
            others.append(block[at - low : at - low + 1, :].astype(jnp.float32) * mate_step)
        table_ref[r, :, :] = jnp.concatenate(rows, axis=0).astype(jnp.bfloat16)
        table_ref[2 + r, :, :] = surf_ref[r, :, :].astype(jnp.bfloat16)
        table_ref[4 + r, :, :] = jnp.concatenate(others, axis=0).astype(jnp.bfloat16)


def swap_inner(x, place):
    return jnp.where(place == 1, roll(x, -1), jnp.where(place == 2, roll(x, 1), x))


def interior_kernel(x_ref, link_ref, mate_ref, spread_ref, near_ref, rows_ref, rate_ref):
    del near_ref
    link_step, mate_step = step_of(link_ref), step_of(mate_ref)
    lane = lane_index(LEV)
    rates = jnp.zeros((LEV, LANES), jnp.float32)
    for v in range(VARS):
        rates = jnp.where(lane // 16 == v, spread_ref[v * LEV : (v + 1) * LEV, :], rates)
    rate_ref[...] = rates
    for v in range(VARS):
        block = slice(v * LEV, (v + 1) * LEV)
        field = [
            decode_block(link_ref, 1, v, link_step),
            decode_block(link_ref, 0, v, link_step),
            x_ref[pl.ds(2 * LEV * v + side(), LEV, stride=2), :],
            x_ref[pl.ds(2 * LEV * v + 1 - side(), LEV, stride=2), :],
            decode_block(mate_ref, 1, v, mate_step),
            decode_block(mate_ref, 0, v, mate_step),
        ]
        rate = spread_ref[block, :]
        for ri in range(4):
            center = field[ri + 1]
            left = jnp.where(lane == 0, 0.0, roll(center, 1))
            right = jnp.where(lane == LANES - 1, 0.0, roll(center, -1))
            rows_ref[ri, block, :] = center + rate * (
                field[ri + 2] + field[ri] + right + left - 4.0 * center
            )


def first_kernel(
    rows_ref, full_ref, recv_ref, rate_ref, spread_ref, op_ref, center_ref, rounded_ref, rhs, out_ref
):
    lane = lane_index(LEV)
    place = lane % 4
    halo = unfold(recv_ref[...].astype(jnp.float32))
    own = full_ref[...]
    beside = jnp.where(place == 1, roll(halo, 1) + roll(own, -1), roll(own, 1) + roll(halo, -1))
    corner = halo + rate_ref[...] * (roll(halo, 4) + roll(halo, -4) + beside - 4.0 * halo)
    corner = swap_inner(corner, place)
    halo = swap_inner(halo * rate_ref[...], place)
    ends = (lane == 0) | (lane == LANES - 1)
    for v in range(VARS):
        block = slice(v * LEV, (v + 1) * LEV)
        for ri in range(4):
            beyond = jnp.where(ends, roll(halo, 126 - 16 * v - 4 * ri), 0.0)
            center = rows_ref[ri, block, :] + beyond
            out_ref[ri, block, :] = center
            rhs[block, ri * LANES : (ri + 1) * LANES] = center.astype(jnp.bfloat16)
        moved = roll(corner, -16 * v)
        out_ref[4, block, :] = moved
        rhs[block, 4 * LANES :] = moved.astype(jnp.bfloat16)
    for ri in range(0, 5, 2):
        width = min(2, 5 - ri)
        tendency = jnp.dot(
            op_ref[0],
            rhs[:, ri * LANES : (ri + width) * LANES],
            preferred_element_type=jnp.float32,
        )
        for k in range(width):
            out_ref[ri + k] += tendency[:, k * LANES : (k + 1) * LANES]
    second_stencil(out_ref, spread_ref, center_ref, rounded_ref)


def decode_block(msg_ref, r, v, step):
    at = r * VL + v * LEV
    low = at // 16 * 16
    block = msg_ref[low : low + 80, :].astype(jnp.int32).astype(jnp.float32)
    return block[at - low : at - low + LEV, :] * step


def second_stencil(field_ref, spread_ref, center_ref, rounded_ref):
    lane = lane_index(LEV)
    place = side()
    for v in range(VARS):
        block = slice(v * LEV, (v + 1) * LEV)
        rate = spread_ref[block, :]
        field = [field_ref[ri, block, :] for ri in range(5)]
        for r in range(2):
            ri = r + 1
            center = field[ri]
            ends = roll(field[4], 126 - 4 * ri)
            left = jnp.where(lane == 0, ends, roll(center, 1))
            right = jnp.where(lane == LANES - 1, ends, roll(center, -1))
            center = center + rate * (field[ri + 1] + field[ri - 1] + right + left - 4.0 * center)
            at = 2 * LEV * v + (place if r == 0 else 1 - place)
            center_ref[pl.ds(at, LEV, stride=2), :] = center
            rounded_ref[block, r * LANES : (r + 1) * LANES] = center.astype(jnp.bfloat16)


def second_kernel(
    center_ref, rounded_ref, op_ref, weight_ref, near_ref, far_ref, entry_ref, pick_ref, count_ref,
    out_hbm, out_ref, sems,
):
    fluxes = [
        flux_of(r, weight_ref, near_ref, far_ref, entry_ref, pick_ref, count_ref) for r in range(2)
    ]
    place = side()
    copies = []
    for i, (low, high) in enumerate(PARTS):
        size = (high - low) * LEV
        tendency = jnp.dot(
            op_ref[0, low * LEV : high * LEV, :],
            rounded_ref[...],
            preferred_element_type=jnp.float32,
        )
        for r in range(2):
            rows = pl.ds(2 * LEV * low + (place if r == 0 else 1 - place), size, stride=2)
            out_ref[rows, :] = center_ref[rows, :] + tendency[:, r * LANES : (r + 1) * LANES]
        for v in range(low, high):
            for r in range(2):
                at = 2 * LEV * v + r
                out_ref[at : at + 1, :] = out_ref[at : at + 1, :] + fluxes[r][v : v + 1, :]
        rows = pl.ds(2 * LEV * low, 2 * size)
        copies.append(pltpu.make_async_copy(out_ref.at[rows, :], out_hbm.at[rows, :], sems.at[i]))
        copies[i].start()
    for copy in copies:
        copy.wait()


def flux_of(r, weight_ref, near_ref, far_ref, entry_ref, pick_ref, count_ref):
    mine = lax.axis_index("sec")
    blocks, weights = [], []
    for slot in range(4):
        entry = entry_ref[0, r, 0, slot]
        apart = mine ^ (entry // 6)
        within = entry % 6
        within = jnp.where(side() == 0, within, 5 - within)
        block = jnp.where(
            apart == 2, near_ref[within], far_ref[jnp.where(apart == 3, 6, 0) + within]
        )
        blocks.append(jnp.where(slot < count_ref[0, r], block, jnp.zeros_like(block)))
        weights.append(weight_ref[pick_ref[0, r, 0, slot]])
    blocks, weights = jnp.concatenate(blocks, axis=1), jnp.concatenate(weights, axis=0)
    return 0.5 * jnp.dot(blocks, weights, preferred_element_type=jnp.float32)


def call(kernel, outs, specs, scratch=(), flops=0, moved=0, out_specs=None):
    return pl.pallas_call(
        kernel,
        out_shape=[jax.ShapeDtypeStruct(shape, dtype) for shape, dtype in outs],
        in_specs=specs,
        out_specs=out_specs or [VMEM] * len(outs),
        scratch_shapes=list(scratch),
        compiler_params=pltpu.CompilerParams(vmem_limit_bytes=40 * 2**20),
        cost_estimate=pl.CostEstimate(flops=flops, bytes_accessed=moved, transcendentals=0),
    )


def solution(mesh):
    sections, tiles, cols = (mesh.shape[a] for a in AXES)

    def send(x, move):
        def index(s, t, c):
            return (s * tiles + t) * cols + c

        pairs = [
            (index(s, t, c), index(*move(s, t, c)))
            for s in range(sections)
            for t in range(tiles)
            for c in range(cols)
        ]
        return lax.ppermute(x, AXES, pairs)

    def shards(state, column_op, diffusion, remap_weights, source_rows, weight_index, counts):
        x = state.reshape(2 * VL, LANES)
        wide, narrow = ((LEV, LANES), jnp.float32), ((LEV - FOLD, LANES), jnp.bfloat16)
        to_link, to_mate = call(
            encode_kernel,
            [((2 * VL + 2 * TAIL, LANES), jnp.int16), ((2 * VL + TAIL, LANES), jnp.int16)],
            [VMEM],
            moved=10**6,
        )(x)
        link = send(to_link, lambda s, t, c: (s, (t - 1 + 2 * (t % 2)) % tiles, c))
        mate = send(to_mate, lambda s, t, c: (s, t + 1 - 2 * (t % 2), c))
        edge, surf, spread = call(
            own_kernel,
            [wide, ((2, VARS, LANES), jnp.float32), ((VL, LANES), jnp.float32)],
            [VMEM] * 2,
            moved=10**6,
        )(x, diffusion)
        full, full16, table = call(
            pack_kernel,
            [wide, narrow, ((6, VARS, LANES), jnp.bfloat16)],
            [VMEM] * 4,
            moved=10**6,
        )(link, mate, edge, surf)
        near = send(table, lambda s, t, c: (s ^ 2, t, c))
        recv = send(full16, lambda s, t, c: (s, t, 1 - c))
        both = jnp.concatenate([table, near], axis=0)
        far = send(both, lambda s, t, c: (s ^ 1, t, c))
        inner, rates = call(
            interior_kernel,
            [((4, VL, LANES), jnp.float32), wide],
            [VMEM] * 5,
            moved=3 * 10**6,
        )(x, link, mate, spread, near)
        center, rounded = call(
            first_kernel,
            [((2 * VL, LANES), jnp.float32), ((VL, 2 * LANES), jnp.bfloat16)],
            [VMEM] * 6,
            [
                pltpu.VMEM((VL, 5 * LANES), jnp.bfloat16),
                pltpu.VMEM((5, VL, LANES), jnp.float32),
            ],
            flops=2 * VL * VL * 5 * LANES,
            moved=2 * 10**6,
        )(inner, full, recv, rates, spread, column_op)
        (out,) = call(
            second_kernel,
            [((2 * VL, LANES), jnp.float32)],
            [VMEM] * 6 + [SMEM] * 3,
            [
                pltpu.VMEM((2 * VL, LANES), jnp.float32),
                pltpu.SemaphoreType.DMA((len(PARTS),)),
            ],
            flops=2 * VL * VL * 2 * LANES,
            moved=2 * 10**6,
            out_specs=[HBM],
        )(center, rounded, column_op, remap_weights, near, far, source_rows, weight_index, counts.reshape(1, 2))
        return out.reshape(1, VARS, LEV, 2, LANES)

    in_specs = (
        P("sec", None, None, "tile", "col"),
        P("sec", None, None),
        P("sec", None),
        P(),
        P("sec", "tile", "col", None),
        P("sec", "tile", "col", None),
        P("sec", "tile", "col"),
    )
    out_specs = P("sec", None, None, "tile", "col")
    return jax.shard_map(shards, mesh=mesh, in_specs=in_specs, out_specs=out_specs, check_vma=False)
```
